32 devices in a mesh: cfg: 2 (over core), tower: 4 (over z), seq: 4 (over y, x).
Axes of the slice: x: 2, y: 2, z: 4, core: 2. Of those that a mesh axis runs over, the one named last changes fastest.
Arguments:
- query_self: bfloat16 [2, 256, 2048], P('cfg', ('tower', 'seq')), may hold values from -320 to 320
- query_cross: bfloat16 [2, 256, 2048], P('cfg', ('tower', 'seq')), may hold values from -320 to 320
- key_vectors: bfloat16 [2, 256, 2048], P('cfg', ('tower', 'seq')), may hold values from -13 to 13
- values: bfloat16 [2, 256, 2048], P('cfg', ('tower', 'seq')), may hold values from -6 to 6
- positions: int32 [256], P(('tower', 'seq')), may hold values from 0 to 155, as said below
- counts: int32 [16], replicated, may hold values from 8 to 16, as said below
- guidance: float32 [1], replicated, may hold values from 1.5 to 3.5
Outputs:
- guided: bfloat16 [256, 2048], P(('tower', 'seq'), 'cfg')
The draws below stay inside these ranges and needn't reach their ends.
Inputs may be any that keep to these rules, and one draw needn't show every extreme that they name: `positions`: integer times on one clock for video and audio tokens, never falling along the video tokens and along the audio tokens; the video tokens of one latent frame share a time. `counts`: valid tokens of each device; a device's slots beyond its count are padding.
All inputs are finite; a program needn't handle non-finite values.
Results may differ from the reference program's by a relative error of at most 0.029.
Values may be sent and summed in bfloat16 or wider, within the bound.
No kernel may reach another device: no remote copies, remote signals or barrier semaphores. Data moves between devices by JAX's collectives and lax.ppermute only.
A program may use at most 64 MiB of HBM per device.

```python
import math
import jax
import jax.numpy as jnp
from jax import lax

HEADS = 16
DHEAD = 128
TOK_DEV = 16
FRAMES = 32
LV = 192
LA = 64
TOKENS = 256
N_TOWER = 4
N_SEQ = 4


def rotate_by(matrix, delta):
    half_dim = DHEAD // 2
    frequency = 10000.0 ** (-(jnp.arange(half_dim, dtype=jnp.float32) * 2.0 / DHEAD))
    angles = delta.astype(jnp.float32)[:, None] * frequency[None, :]
    cosine = jnp.cos(angles)[None, :, None, :]
    sine_part = jnp.sin(angles)[None, :, None, :]
    heads_f32 = matrix.reshape(2, TOKENS, HEADS, DHEAD)
    front_half = heads_f32[..., :half_dim]
    back_half = heads_f32[..., half_dim:]
    rotated = jnp.concatenate([front_half * cosine - back_half * sine_part, back_half * cosine + front_half * sine_part], axis=-1)
    return rotated.reshape(2, TOKENS, HEADS * DHEAD)


def shared_draws(key, emphasis):
    frame_steps = jax.random.randint(jax.random.fold_in(key, 1), (FRAMES,), 3, 6)
    frame_time = jnp.cumsum(frame_steps) - frame_steps[0]
    frame_index = jnp.arange(FRAMES, dtype=jnp.int32)
    frame_time = jnp.where(frame_index == FRAMES - 1, 5 * (FRAMES - 1), frame_time)
    video_index = jnp.arange(LV, dtype=jnp.int32)
    video_time = frame_time[video_index // (LV // FRAMES)]
    audio_index = jnp.arange(LA, dtype=jnp.int32)
    audio_time = audio_index * frame_time[FRAMES - 1] // LA + jax.random.randint(jax.random.fold_in(key, 2), (LA,), 0, 2)
    audio_time = jax.lax.cummax(audio_time.astype(jnp.int32), axis=0)
    positions = jnp.concatenate([video_time, audio_time]).astype(jnp.int32)
    shape = (2, TOKENS, HEADS * DHEAD)
    self_base = jnp.clip(jax.random.normal(jax.random.fold_in(key, 3), shape, jnp.float32), -6.0, 6.0) * 1.5
    cross_base = jnp.clip(jax.random.normal(jax.random.fold_in(key, 4), shape, jnp.float32), -6.0, 6.0) * 1.5
    key_base = jnp.clip(jax.random.normal(jax.random.fold_in(key, 5), shape, jnp.float32), -6.0, 6.0) * 1.5
    chosen = jax.random.randint(jax.random.fold_in(key, 6), (TOKENS,), 0, 32) == 0
    strength = (12 + 4 * jax.random.randint(jax.random.fold_in(key, 7), (TOKENS,), 0, 4)).astype(jnp.float32)
    token_index = jnp.arange(TOKENS, dtype=jnp.int32)
    active = emphasis > 0.0
    before_index = jnp.maximum(token_index - 1, 0)
    lifted = rotate_by(key_base[:, before_index], positions[before_index] - positions) * (1.0 + 0.08 / strength[before_index])[None, :, None]
    second_use = (token_index % 2 == 1) & chosen[before_index] & active
    key_final = jnp.where(second_use[None, :, None], lifted, key_base)
    self_use = (token_index % 4 == 0) & chosen & active
    query_self = jnp.where(self_use[None, :, None], emphasis * strength[None, :, None] * key_base, self_base)
    partner = jnp.where(token_index < LV, LV + token_index % LA, token_index - LV)
    cross_use = (token_index % 4 == 2) & chosen[partner] & active
    aimed = rotate_by(key_base[:, partner], positions[partner] - positions) * (emphasis * strength[partner])[None, :, None]
    query_cross = jnp.where(cross_use[None, :, None], aimed, cross_base)
    return (positions, query_self, query_cross, key_final)


def draw_query_self(key, part):
    emphasis = 0.0
    return shared_draws(key, emphasis)[1].astype(jnp.bfloat16)


def draw_query_cross(key, part):
    emphasis = 0.0
    return shared_draws(key, emphasis)[2].astype(jnp.bfloat16)


def draw_key_vectors(key, part):
    emphasis = 0.0
    return shared_draws(key, emphasis)[3].astype(jnp.bfloat16)


def draw_positions(key, part):
    return shared_draws(key, 0.0)[0]


def draw_counts(key, part):
    key = jax.random.fold_in(key, 41)
    device_count = N_TOWER * N_SEQ
    drawn = jax.random.randint(jax.random.fold_in(key, 1), (device_count,), TOK_DEV // 2, TOK_DEV + 1)
    full_at = jax.random.randint(jax.random.fold_in(key, 2), (), 0, device_count)
    return jnp.where(jnp.arange(device_count, dtype=jnp.int32) == full_at, TOK_DEV, drawn).astype(jnp.int32)


def level_of(own_key, extent, cuts, least, largest):
    gain, own = 1.0, jax.random.fold_in(own_key, 6)
    for dim, shards_of in cuts:
        steps = jnp.exp(jax.random.uniform(jax.random.fold_in(own, dim), (shards_of,), jnp.float32, least / len(cuts), largest / len(cuts)))
        gain = gain * jnp.repeat(steps, extent[dim] // shards_of).reshape([-1 if axis == dim else 1 for axis in range(len(extent))])
    return gain


def scatter_about(key, extent, spread, limit, cuts=(), held_as=jnp.bfloat16):
    entries = jax.random.normal(key, extent, jnp.float32) * spread
    if len(cuts) > 0:
        entries = level_of(key, extent, cuts, -0.22, 0.18) * entries
    return jnp.clip(entries, min=-limit, max=limit).astype(held_as)


def setup_inputs(seed: int = 0) -> dict:
    seeds = jax.random.split(jax.random.key(seed), 8)
    return {
        "query_self": draw_query_self(jax.random.fold_in(seeds[7], 71), 0),
        "query_cross": draw_query_cross(jax.random.fold_in(seeds[7], 71), 0),
        "key_vectors": draw_key_vectors(jax.random.fold_in(seeds[7], 71), 0),
        "values": scatter_about(seeds[3], (2, TOKENS, HEADS * DHEAD), 1.0, 6.0, ((0, 2), (1, 16))),
        "positions": draw_positions(jax.random.fold_in(seeds[7], 71), 0),
        "counts": draw_counts(jax.random.fold_in(seeds[7], 71), 0),
        "guidance": jnp.clip(jax.random.uniform(seeds[6], (1,), jnp.float32, 1.5, 3.5), 1.5, 3.5),
    }


def rotate_heads(matrix, positions):
    token_count = matrix.shape[0]
    half_dim = DHEAD // 2
    frequency = 10000.0 ** (-(jnp.arange(half_dim, dtype=jnp.float32) * 2.0 / DHEAD))
    angles = positions.astype(jnp.float32)[:, None] * frequency[None, :]
    cosine = jnp.cos(angles)[:, None, :]
    sine_part = jnp.sin(angles)[:, None, :]
    heads_f32 = matrix.astype(jnp.float32).reshape(token_count, HEADS, DHEAD)
    front_half = heads_f32[..., :half_dim]
    back_half = heads_f32[..., half_dim:]
    rotated = jnp.concatenate([front_half * cosine - back_half * sine_part, back_half * cosine + front_half * sine_part], axis=-1)
    return rotated.reshape(token_count, HEADS * DHEAD).astype(jnp.bfloat16)

def attend_all(queries, key_rows, value_rows, key_valid):
    query_count = queries.shape[0]
    block_size = math.gcd(query_count, 512)
    scale_factor = 1.0 / math.sqrt(DHEAD)

    def one_head(head_at):
        start = head_at * DHEAD
        head_query = lax.dynamic_slice_in_dim(queries, start, DHEAD, 1).reshape(query_count // block_size, block_size, DHEAD)
        head_keys = lax.dynamic_slice_in_dim(key_rows, start, DHEAD, 1)
        head_values = lax.dynamic_slice_in_dim(value_rows, start, DHEAD, 1)

        def one_block(query_rows):
            scores = jnp.dot(query_rows, head_keys.T, preferred_element_type=jnp.float32) * scale_factor
            scores = jnp.where(key_valid[None, :], scores, -jnp.inf)
            highest = lax.optimization_barrier(jnp.max(scores, axis=1, keepdims=True))
            weights = jnp.where(key_valid[None, :], jnp.exp(scores - highest), 0.0)
            weight_sum = lax.optimization_barrier(jnp.sum(weights, axis=1, keepdims=True))
            return jnp.dot(weights.astype(jnp.bfloat16), head_values, preferred_element_type=jnp.float32) / weight_sum
        return lax.map(one_block, head_query).reshape(query_count, DHEAD)
    per_head = lax.map(one_head, jnp.arange(HEADS, dtype=jnp.int32))
    return jnp.transpose(per_head, (1, 0, 2)).reshape(query_count, HEADS * DHEAD)

def reference(query_self, query_cross, key_vectors, values, positions, counts, guidance):
    token_index = jnp.arange(TOKENS, dtype=jnp.int32)
    valid = token_index % TOK_DEV < counts[token_index // TOK_DEV]
    normed_list = []
    for branch in range(2):
        rot_self = rotate_heads(query_self[branch], positions)
        rot_cross = rotate_heads(query_cross[branch], positions)
        rot_keys = rotate_heads(key_vectors[branch], positions)
        value_rows = values[branch]
        video_self = attend_all(rot_self[:LV], rot_keys[:LV], value_rows[:LV], valid[:LV])
        video_cross = attend_all(rot_cross[:LV], rot_keys[LV:], value_rows[LV:], valid[LV:])
        audio_self = attend_all(rot_self[LV:], rot_keys[LV:], value_rows[LV:], valid[LV:])
        audio_cross = attend_all(rot_cross[LV:], rot_keys[:LV], value_rows[:LV], valid[:LV])
        combined = jnp.concatenate([video_self + video_cross, audio_self + audio_cross], axis=0)
        combined = jnp.where(valid[:, None], combined, 0.0).astype(jnp.bfloat16)
        block_f32 = combined.astype(jnp.float32)
        scale_rows = lax.rsqrt(lax.optimization_barrier(jnp.mean(block_f32 * block_f32, axis=1, keepdims=True)) + 1e-06)
        normed_list.append((block_f32 * scale_rows).astype(jnp.bfloat16))
    conditional = normed_list[0].astype(jnp.float32)
    unconditional = normed_list[1].astype(jnp.float32)
    guided = unconditional + guidance[0] * (conditional - unconditional)
    return guided.astype(jnp.bfloat16)
```

```python
import functools
import math

import jax
import jax.numpy as jnp
from jax import lax
from jax.experimental import pallas as pl
from jax.experimental.pallas import tpu as pltpu
from jax.sharding import PartitionSpec as P

HEADS = 16
DHEAD = 128
EXPONENT_SCALE = math.log2(math.e) / math.sqrt(DHEAD)
VMEM_LIMIT = 32 * 1024 * 1024


def rotate_kernel(video_keys, positions_hbm, counts_hbm, *refs):
    sources, (packed_ref, bias_ref, kept_ref) = refs[:4], refs[4:7]
    held, positions_ref, counts_ref, semaphores = refs[7:]
    tokens = held.shape[1]
    copies = [pltpu.make_async_copy(positions_hbm, positions_ref, semaphores.at[4])]
    for part in range(4):
        copies.append(
            pltpu.make_async_copy(sources[part].at[0], held.at[part], semaphores.at[part])
        )
    copies.append(pltpu.make_async_copy(counts_hbm, counts_ref, semaphores.at[5]))
    for copy in copies:
        copy.start()
    copies[0].wait()
    row = lax.broadcasted_iota(jnp.int32, (tokens, DHEAD), 0)
    lane = lax.broadcasted_iota(jnp.int32, (tokens, DHEAD), 1)
    time = jnp.zeros((tokens, DHEAD), jnp.int32)
    for token in range(tokens):
        time = jnp.where(row == token, positions_ref[token], time)
    half = DHEAD // 2
    index = (lane % half).astype(jnp.float32)
    angles = time.astype(jnp.float32) * jnp.exp(index * (-2.0 * math.log(10000.0) / DHEAD))
    cosine = jnp.cos(angles)
    sine = jnp.where(lane < half, -jnp.sin(angles), jnp.sin(angles))
    for part in range(4):
        copies[1 + part].wait()
        for head in range(HEADS):
            columns = held[part, :, head * DHEAD : (head + 1) * DHEAD]
            if part < 3:
                columns = columns.astype(jnp.float32)
                columns = columns * cosine + pltpu.roll(columns, half, 1) * sine
            packed_ref[head, part] = columns.astype(jnp.bfloat16)
    copies[5].wait()
    devices = counts_ref.shape[0]
    limits = [counts_ref[device] for device in range(devices)]
    key = lax.broadcasted_iota(jnp.int32, bias_ref.shape, 1)
    past = jnp.zeros(bias_ref.shape, jnp.int32)
    for device in range(devices):
        first = device * tokens
        past = jnp.where(key >= first, first + limits[device], past)
    is_audio = (key >= video_keys).astype(jnp.int32)
    modality = lax.broadcasted_iota(jnp.int32, bias_ref.shape, 0)
    bias_ref[...] = jnp.where((key < past) & (is_audio == modality), 0.0, -1e30)
    block_rows = kept_ref.shape[0] // devices
    slot = lax.broadcasted_iota(jnp.int32, (block_rows, DHEAD), 0)
    if block_rows < tokens:
        part = lax.rem(lax.axis_index(("tower", "seq")), tokens // block_rows)
        slot += part * block_rows
    for device in range(devices):
        rows = pl.ds(device * block_rows, block_rows)
        kept_ref[rows, :] = jnp.where(slot < limits[device], 1.0, 0.0)


def attend(queries, keys, values, bias):
    scores = lax.dot_general(
        queries, keys, (((1,), (1,)), ((), ())), preferred_element_type=jnp.float32
    )
    scores = scores + bias
    weights = jnp.exp2((scores - jnp.max(scores, axis=1, keepdims=True)) * EXPONENT_SCALE)
    both = jnp.dot(
        weights.astype(jnp.bfloat16),
        jnp.concatenate([values, jnp.ones_like(values)], axis=1),
        preferred_element_type=jnp.float32,
    )
    return both[:, :DHEAD], both[:, DHEAD:]


def attend_kernel(n_tower, ranks, bias_ref, kept_ref, *refs):
    out_ref = refs[-1]
    devices, block_rows, _ = out_ref.shape
    if len(refs) == 2:
        q_self, q_cross, keys, values = (
            jnp.concatenate([refs[0][rank, part] for rank in ranks[0]], axis=0)
            for part in range(4)
        )
    else:
        q_self, q_cross, keys, values = (ref[...] for ref in refs[:4])
    video_keys = keys.shape[0] // n_tower * (n_tower - 1)
    video_queries = q_self.shape[0] // n_tower * (n_tower - 1)
    to_video = jnp.concatenate([q_self[:video_queries], q_cross[video_queries:]], axis=0)
    to_audio = jnp.concatenate([q_cross[:video_queries], q_self[video_queries:]], axis=0)
    last_video = pl.cdiv(video_keys, DHEAD) * DHEAD
    first_audio = video_keys // DHEAD * DHEAD
    video, video_sum = attend(
        to_video, keys[:last_video], values[:last_video], bias_ref[0:1, :last_video]
    )
    audio, audio_sum = attend(
        to_audio, keys[first_audio:], values[first_audio:], bias_ref[1:2, first_audio:]
    )
    combined = video * audio_sum + audio * video_sum
    combined = (combined * (kept_ref[...] / (video_sum * audio_sum))).astype(jnp.bfloat16)
    for device in range(devices):
        out_ref[ranks[1][device]] = combined[device * block_rows : (device + 1) * block_rows]


def norm_kernel(head_ranks, blocks_ref, kept_ref, sent_ref):
    heads, tokens, _ = blocks_ref.shape
    half_heads = heads // 2
    core = lax.axis_index("cfg")
    total = jnp.zeros((tokens, DHEAD), jnp.float32)
    for head in range(heads):
        block = blocks_ref[head].astype(jnp.float32)
        total += block * block
    mean = jnp.sum(total, axis=1, keepdims=True) * (1.0 / (heads * DHEAD))
    scale = lax.rsqrt(mean + 1e-6)
    for at in range(half_heads):
        low, high = head_ranks[at], head_ranks[half_heads + at]
        for rank, target in (
            (jnp.where(core == 0, low, high), kept_ref),
            (jnp.where(core == 0, high, low), sent_ref),
        ):
            normed = blocks_ref[rank].astype(jnp.float32) * scale
            target[:, at * DHEAD : (at + 1) * DHEAD] = normed.astype(jnp.bfloat16)


def guide_kernel(guidance_ref, kept_ref, met_ref, out_ref):
    kept, met = kept_ref[...].astype(jnp.float32), met_ref[...].astype(jnp.float32)
    first = lax.axis_index("cfg") == 0
    conditional, unconditional = jnp.where(first, kept, met), jnp.where(first, met, kept)
    guided = unconditional + guidance_ref[0] * (conditional - unconditional)
    out_ref[...] = guided.astype(jnp.bfloat16)


def local_call(kernel, out_shape, in_spaces, arrays, scratch=()):
    out_spec = pl.BlockSpec(memory_space=pltpu.VMEM)
    return pl.pallas_call(
        kernel,
        out_shape=out_shape,
        in_specs=[pl.BlockSpec(memory_space=space) for space in in_spaces],
        out_specs=[out_spec] * len(out_shape) if isinstance(out_shape, list) else out_spec,
        scratch_shapes=scratch,
        compiler_params=pltpu.CompilerParams(vmem_limit_bytes=VMEM_LIMIT),
    )(
        *(
            pltpu.with_memory_space_constraint(array, space) if space == pltpu.HBM else array
            for array, space in zip(arrays, in_spaces)
        )
    )


def per_device(query_self, query_cross, key_vectors, values, positions, counts, guidance):
    n_tower, n_seq = lax.axis_size("tower"), lax.axis_size("seq")
    devices = n_tower * n_seq
    tokens, features = query_self.shape[1:]
    query_blocks = devices // HEADS
    block_rows = tokens // query_blocks
    video_keys = (n_tower - 1) * n_seq * tokens
    spreading, collecting = list(range(devices)), list(range(devices))
    if query_blocks == 1:
        spreading = spreading[-1:] + spreading[:-1]
        collecting = collecting[-1:] + collecting[:-1]
    ranks = [[order.index(device) for device in range(devices)] for order in (spreading, collecting)]

    def exchange(array, order):
        return lax.all_to_all(
            array,
            ("tower", "seq"),
            split_axis=0,
            concat_axis=0,
            tiled=True,
            axis_index_groups=[order],
        )

    packed, bias, kept_rows = local_call(
        functools.partial(rotate_kernel, video_keys),
        [
            pltpu.VMEM((HEADS, 4, tokens, DHEAD), jnp.bfloat16),
            pltpu.VMEM((2, devices * tokens), jnp.float32),
            pltpu.VMEM((devices * block_rows, DHEAD), jnp.float32),
        ],
        [pltpu.HBM] * 6,
        (positions, counts, query_self, query_cross, key_vectors, values),
        [
            pltpu.VMEM((4, tokens, features), jnp.bfloat16),
            pltpu.SMEM((tokens,), jnp.int32),
            pltpu.SMEM((devices,), jnp.int32),
            pltpu.SemaphoreType.DMA((6,)),
        ],
    )
    if query_blocks == 1:
        arrived = [exchange(packed, spreading)]
    else:
        queries = packed[:, :2].reshape(HEADS, 2, query_blocks, block_rows, DHEAD)
        queries = queries.transpose(0, 2, 1, 3, 4).reshape(devices, 2, block_rows, DHEAD)
        spread = jnp.broadcast_to(packed[:, None, 2:], (HEADS, query_blocks, 2, tokens, DHEAD))
        spread = spread.reshape(devices, 2, tokens, DHEAD)
        arrived = [
            exchange(part, spreading).transpose(1, 0, 2, 3).reshape(2, -1, DHEAD)
            for part in (queries, spread)
        ]
        arrived = [part[at] for part in arrived for at in range(2)]
    blocks = local_call(
        functools.partial(attend_kernel, n_tower, ranks),
        pltpu.VMEM((devices, block_rows, DHEAD), jnp.bfloat16),
        [pltpu.VMEM] * (2 + len(arrived)),
        (bias, kept_rows, *arrived),
    )
    half = (tokens, features // 2)
    returned = exchange(blocks, collecting).reshape(HEADS, tokens, DHEAD)
    workers = spreading if query_blocks == 1 else list(range(HEADS))
    kept, sent = local_call(
        functools.partial(norm_kernel, [ranks[1][worker] for worker in workers]),
        [pltpu.VMEM(half, jnp.bfloat16)] * 2,
        [pltpu.VMEM],
        (returned,),
    )
    met = lax.ppermute(sent, "cfg", [(0, 1), (1, 0)])
    return local_call(
        guide_kernel,
        jax.ShapeDtypeStruct(half, jnp.bfloat16),
        [pltpu.SMEM, pltpu.VMEM, pltpu.VMEM],
        (guidance, kept, met),
    )


def solution(mesh):
    return jax.shard_map(
        per_device,
        mesh=mesh,
        in_specs=(
            P("cfg", ("tower", "seq"), None),
            P("cfg", ("tower", "seq"), None),
            P("cfg", ("tower", "seq"), None),
            P("cfg", ("tower", "seq"), None),
            P(("tower", "seq")),
            P(),
            P(),
        ),
        out_specs=P(("tower", "seq"), "cfg"),
        check_vma=False,
    )
```

```python
import functools
import math

import jax
import jax.numpy as jnp
from jax import lax
from jax.experimental import pallas as pl
from jax.experimental.pallas import tpu as pltpu
from jax.sharding import PartitionSpec as P

HEADS = 16
DHEAD = 128
EXPONENT_SCALE = math.log2(math.e) / math.sqrt(DHEAD)
VMEM_LIMIT = 32 * 1024 * 1024


def sine_and_cosine(angles):
    turns = jnp.floor(angles * (2.0 / math.pi) + 0.5)
    rest = angles - turns * 1.5703125
    rest = rest - turns * 4.837512969970703e-4
    rest = rest - turns * 7.549789954891882e-8
    square = rest * rest
    sine = (-1.9515295891e-4 * square + 8.3321608736e-3) * square - 1.6666654611e-1
    sine = rest + rest * square * sine
    cosine = (2.443315711809948e-5 * square - 1.388731625493765e-3) * square
    cosine = 1.0 - 0.5 * square + square * square * (cosine + 4.166664568298827e-2)
    quarter = turns.astype(jnp.int32)
    odd = (quarter & 1) == 1
    sine, cosine = jnp.where(odd, cosine, sine), jnp.where(odd, sine, cosine)
    sine = jnp.where((quarter & 2) == 2, -sine, sine)
    cosine = jnp.where(((quarter + 1) & 2) == 2, -cosine, cosine)
    return sine, cosine


def rotate_kernel(video_keys, positions_hbm, counts_hbm, *refs):
    sources, (packed_ref, bias_ref, kept_ref) = refs[:4], refs[4:7]
    held, positions_ref, counts_ref, semaphores = refs[7:]
    tokens = held.shape[1]
    copies = [
        pltpu.make_async_copy(sources[part].at[0], held.at[part], semaphores.at[part])
        for part in range(4)
    ]
    copies.append(pltpu.make_async_copy(positions_hbm, positions_ref, semaphores.at[4]))
    copies.append(pltpu.make_async_copy(counts_hbm, counts_ref, semaphores.at[5]))
    for copy in copies:
        copy.start()
    copies[4].wait()
    row = lax.broadcasted_iota(jnp.int32, (tokens, DHEAD), 0)
    lane = lax.broadcasted_iota(jnp.int32, (tokens, DHEAD), 1)
    time = jnp.zeros((tokens, DHEAD), jnp.int32)
    for token in range(tokens):
        time = jnp.where(row == token, positions_ref[token], time)
    half = DHEAD // 2
    index = (lane % half).astype(jnp.float32)
    angles = time.astype(jnp.float32) * jnp.exp(index * (-2.0 * math.log(10000.0) / DHEAD))
    sine, cosine = sine_and_cosine(angles)
    sine = jnp.where(lane < half, -sine, sine)
    for copy in copies[:4] + copies[5:]:
        copy.wait()
    for part in range(4):
        for head in range(HEADS):
            columns = held[part, :, head * DHEAD : (head + 1) * DHEAD]
            if part < 3:
                columns = columns.astype(jnp.float32)
                columns = columns * cosine + pltpu.roll(columns, half, 1) * sine
            packed_ref[head, part * tokens : (part + 1) * tokens] = columns.astype(jnp.bfloat16)
    devices = counts_ref.shape[0]
    limits = [counts_ref[device] for device in range(devices)]
    key = lax.broadcasted_iota(jnp.int32, bias_ref.shape, 1)
    past = jnp.zeros(bias_ref.shape, jnp.int32)
    for device in range(devices):
        first = device * tokens
        past = jnp.where(key >= first, first + limits[device], past)
    is_audio = (key >= video_keys).astype(jnp.int32)
    modality = lax.broadcasted_iota(jnp.int32, bias_ref.shape, 0)
    bias_ref[...] = jnp.where((key < past) & (is_audio == modality), 0.0, -1e30)
    block_rows = kept_ref.shape[0] // devices
    slot = lax.broadcasted_iota(jnp.int32, (block_rows, DHEAD), 0)
    if block_rows < tokens:
        part = lax.rem(lax.axis_index(("tower", "seq")), tokens // block_rows)
        slot += part * block_rows
    for device in range(devices):
        rows = pl.ds(device * block_rows, block_rows)
        kept_ref[rows, :] = jnp.where(slot < limits[device], 1.0, 0.0)


def attend(queries, keys, values, bias):
    scores = lax.dot_general(
        queries, keys, (((1,), (1,)), ((), ())), preferred_element_type=jnp.float32
    )
    scores = scores + bias
    weights = jnp.exp2((scores - jnp.max(scores, axis=1, keepdims=True)) * EXPONENT_SCALE)
    both = jnp.dot(
        weights.astype(jnp.bfloat16),
        jnp.concatenate([values, jnp.ones_like(values)], axis=1),
        preferred_element_type=jnp.float32,
    )
    return both[:, :DHEAD], both[:, DHEAD:]


def attend_kernel(n_tower, ranks, bias_ref, kept_ref, *refs):
    out_ref = refs[-1]
    devices, block_rows, _ = out_ref.shape
    if len(refs) == 2:
        q_self, q_cross, keys, values = (
            jnp.concatenate(
                [refs[0][rank, part * block_rows : (part + 1) * block_rows] for rank in ranks[0]],
                axis=0,
            )
            for part in range(4)
        )
    else:
        q_self, q_cross, keys, values = (ref[...] for ref in refs[:4])
    video_keys = keys.shape[0] // n_tower * (n_tower - 1)
    video_queries = q_self.shape[0] // n_tower * (n_tower - 1)
    to_video = jnp.concatenate([q_self[:video_queries], q_cross[video_queries:]], axis=0)
    to_audio = jnp.concatenate([q_cross[:video_queries], q_self[video_queries:]], axis=0)
    last_video = pl.cdiv(video_keys, DHEAD) * DHEAD
    first_audio = video_keys // DHEAD * DHEAD
    video, video_sum = attend(
        to_video, keys[:last_video], values[:last_video], bias_ref[0:1, :last_video]
    )
    audio, audio_sum = attend(
        to_audio, keys[first_audio:], values[first_audio:], bias_ref[1:2, first_audio:]
    )
    combined = video * audio_sum + audio * video_sum
    combined = (combined * (kept_ref[...] / (video_sum * audio_sum))).astype(jnp.bfloat16)
    for device in range(devices):
        out_ref[ranks[1][device]] = combined[device * block_rows : (device + 1) * block_rows]


def norm_kernel(head_ranks, blocks_ref, kept_ref, sent_ref):
    heads, tokens, _ = blocks_ref.shape
    half_heads = heads // 2
    core = lax.axis_index("cfg")
    total = jnp.zeros((tokens, DHEAD), jnp.float32)
    for head in range(heads):
        block = blocks_ref[head].astype(jnp.float32)
        total += block * block
    mean = jnp.sum(total, axis=1, keepdims=True) * (1.0 / (heads * DHEAD))
    scale = lax.rsqrt(mean + 1e-6)
    for at in range(half_heads):
        low, high = head_ranks[at], head_ranks[half_heads + at]
        for rank, target in (
            (jnp.where(core == 0, low, high), kept_ref),
            (jnp.where(core == 0, high, low), sent_ref),
        ):
            normed = blocks_ref[rank].astype(jnp.float32) * scale
            target[:, at * DHEAD : (at + 1) * DHEAD] = normed.astype(jnp.bfloat16)


def guide_kernel(guidance_ref, kept_ref, met_ref, out_ref):
    kept, met = kept_ref[...].astype(jnp.float32), met_ref[...].astype(jnp.float32)
    first = lax.axis_index("cfg") == 0
    conditional, unconditional = jnp.where(first, kept, met), jnp.where(first, met, kept)
    guided = unconditional + guidance_ref[0] * (conditional - unconditional)
    out_ref[...] = guided.astype(jnp.bfloat16)


def local_call(kernel, out_shape, in_spaces, arrays, scratch=()):
    out_spec = pl.BlockSpec(memory_space=pltpu.VMEM)
    return pl.pallas_call(
        kernel,
        out_shape=out_shape,
        in_specs=[pl.BlockSpec(memory_space=space) for space in in_spaces],
        out_specs=[out_spec] * len(out_shape) if isinstance(out_shape, list) else out_spec,
        scratch_shapes=scratch,
        compiler_params=pltpu.CompilerParams(vmem_limit_bytes=VMEM_LIMIT),
    )(
        *(
            pltpu.with_memory_space_constraint(array, space) if space == pltpu.HBM else array
            for array, space in zip(arrays, in_spaces)
        )
    )


def per_device(query_self, query_cross, key_vectors, values, positions, counts, guidance):
    n_tower, n_seq = lax.axis_size("tower"), lax.axis_size("seq")
    devices = n_tower * n_seq
    tokens, features = query_self.shape[1:]
    query_blocks = devices // HEADS
    block_rows = tokens // query_blocks
    video_keys = (n_tower - 1) * n_seq * tokens
    spreading, collecting = list(range(devices)), list(range(devices))
    if query_blocks == 1:
        spreading.reverse()
        middle = devices - n_seq - 1
        collecting = collecting[middle:] + collecting[:middle]
    ranks = [[order.index(device) for device in range(devices)] for order in (spreading, collecting)]

    def exchange(array, order):
        return lax.all_to_all(
            array,
            ("tower", "seq"),
            split_axis=0,
            concat_axis=0,
            tiled=True,
            axis_index_groups=[order],
        )

    packed, bias, kept_rows = local_call(
        functools.partial(rotate_kernel, video_keys),
        [
            pltpu.VMEM((HEADS, 4 * tokens, DHEAD), jnp.bfloat16),
            pltpu.VMEM((2, devices * tokens), jnp.float32),
            pltpu.VMEM((devices * block_rows, DHEAD), jnp.float32),
        ],
        [pltpu.HBM] * 6,
        (positions, counts, query_self, query_cross, key_vectors, values),
        [
            pltpu.VMEM((4, tokens, features), jnp.bfloat16),
            pltpu.SMEM((tokens,), jnp.int32),
            pltpu.SMEM((devices,), jnp.int32),
            pltpu.SemaphoreType.DMA((6,)),
        ],
    )
    if query_blocks == 1:
        arrived = [exchange(packed, spreading)]
    else:
        packed = packed.reshape(HEADS, 4, tokens, DHEAD)
        queries = packed[:, :2].reshape(HEADS, 2, query_blocks, block_rows, DHEAD)
        queries = queries.transpose(0, 2, 1, 3, 4).reshape(devices, 2, block_rows, DHEAD)
        spread = jnp.broadcast_to(packed[:, None, 2:], (HEADS, query_blocks, 2, tokens, DHEAD))
        spread = spread.reshape(devices, 2, tokens, DHEAD)
        arrived = [
            exchange(part, spreading).transpose(1, 0, 2, 3).reshape(2, -1, DHEAD)
            for part in (queries, spread)
        ]
        arrived = [part[at] for part in arrived for at in range(2)]
    blocks = local_call(
        functools.partial(attend_kernel, n_tower, ranks),
        pltpu.VMEM((devices, block_rows, DHEAD), jnp.bfloat16),
        [pltpu.VMEM] * (2 + len(arrived)),
        (bias, kept_rows, *arrived),
    )
    half = (tokens, features // 2)
    returned = exchange(blocks, collecting).reshape(HEADS, tokens, DHEAD)
    workers = spreading if query_blocks == 1 else list(range(HEADS))
    kept, sent = local_call(
        functools.partial(norm_kernel, [ranks[1][worker] for worker in workers]),
        [pltpu.VMEM(half, jnp.bfloat16)] * 2,
        [pltpu.VMEM],
        (returned,),
    )
    met = lax.ppermute(sent, "cfg", [(0, 1), (1, 0)])
    return local_call(
        guide_kernel,
        jax.ShapeDtypeStruct(half, jnp.bfloat16),
        [pltpu.SMEM, pltpu.VMEM, pltpu.VMEM],
        (guidance, kept, met),
    )


def solution(mesh):
    return jax.shard_map(
        per_device,
        mesh=mesh,
        in_specs=(
            P("cfg", ("tower", "seq"), None),
            P("cfg", ("tower", "seq"), None),
            P("cfg", ("tower", "seq"), None),
            P("cfg", ("tower", "seq"), None),
            P(("tower", "seq")),
            P(),
            P(),
        ),
        out_specs=P(("tower", "seq"), "cfg"),
        check_vma=False,
    )
```

```python
import functools
import math

import jax
import jax.numpy as jnp
from jax import lax
from jax.experimental import pallas as pl
from jax.experimental.pallas import tpu as pltpu
from jax.sharding import PartitionSpec as P

HEADS = 16
DHEAD = 128
EXPONENT_SCALE = math.log2(math.e) / math.sqrt(DHEAD)
VMEM_LIMIT = 32 * 1024 * 1024


def rotate_kernel(video_keys, positions_hbm, counts_hbm, *refs):
    sources, (packed_ref, bias_ref, kept_ref) = refs[:4], refs[4:7]
    held, positions_ref, counts_ref, semaphores = refs[7:]
    tokens = held.shape[1]
    copies = [
        pltpu.make_async_copy(sources[part].at[0], held.at[part], semaphores.at[part])
        for part in range(4)
    ]
    copies.append(pltpu.make_async_copy(positions_hbm, positions_ref, semaphores.at[4]))
    copies.append(pltpu.make_async_copy(counts_hbm, counts_ref, semaphores.at[5]))
    for copy in copies:
        copy.start()
    copies[4].wait()
    row = lax.broadcasted_iota(jnp.int32, (tokens, DHEAD), 0)
    lane = lax.broadcasted_iota(jnp.int32, (tokens, DHEAD), 1)
    time = jnp.zeros((tokens, DHEAD), jnp.int32)
    for token in range(tokens):
        time = jnp.where(row == token, positions_ref[token], time)
    half = DHEAD // 2
    index = (lane % half).astype(jnp.float32)
    angles = time.astype(jnp.float32) * jnp.exp(index * (-2.0 * math.log(10000.0) / DHEAD))
    cosine = jnp.cos(angles)
    sine = jnp.where(lane < half, -jnp.sin(angles), jnp.sin(angles))
    for copy in copies[:4] + copies[5:]:
        copy.wait()
    for part in range(4):
        for head in range(HEADS):
            columns = held[part, :, head * DHEAD : (head + 1) * DHEAD]
            if part < 3:
                columns = columns.astype(jnp.float32)
                columns = columns * cosine + pltpu.roll(columns, half, 1) * sine
            packed_ref[head, part * tokens : (part + 1) * tokens] = columns.astype(jnp.bfloat16)
    devices = counts_ref.shape[0]
    limits = [counts_ref[device] for device in range(devices)]
    key = lax.broadcasted_iota(jnp.int32, bias_ref.shape, 1)
    past = jnp.zeros(bias_ref.shape, jnp.int32)
    for device in range(devices):
        first = device * tokens
        past = jnp.where(key >= first, first + limits[device], past)
    is_audio = (key >= video_keys).astype(jnp.int32)
    modality = lax.broadcasted_iota(jnp.int32, bias_ref.shape, 0)
    bias_ref[...] = jnp.where((key < past) & (is_audio == modality), 0.0, -1e30)
    block_rows = kept_ref.shape[0] // devices
    slot = lax.broadcasted_iota(jnp.int32, (block_rows, DHEAD), 0)
    if block_rows < tokens:
        part = lax.rem(lax.axis_index(("tower", "seq")), tokens // block_rows)
        slot += part * block_rows
    for device in range(devices):
        rows = pl.ds(device * block_rows, block_rows)
        kept_ref[rows, :] = jnp.where(slot < limits[device], 1.0, 0.0)


def attend(queries, keys, values, bias):
    scores = lax.dot_general(
        queries, keys, (((1,), (1,)), ((), ())), preferred_element_type=jnp.float32
    )
    scores = scores + bias
    weights = jnp.exp2((scores - jnp.max(scores, axis=1, keepdims=True)) * EXPONENT_SCALE)
    both = jnp.dot(
        weights.astype(jnp.bfloat16),
        jnp.concatenate([values, jnp.ones_like(values)], axis=1),
        preferred_element_type=jnp.float32,
    )
    return both[:, :DHEAD], both[:, DHEAD:]


def attend_kernel(n_tower, ranks, bias_ref, kept_ref, *refs):
    out_ref = refs[-1]
    devices, block_rows, _ = out_ref.shape
    if len(refs) == 2:
        q_self, q_cross, keys, values = (
            jnp.concatenate(
                [refs[0][rank, part * block_rows : (part + 1) * block_rows] for rank in ranks[0]],
                axis=0,
            )
            for part in range(4)
        )
    else:
        q_self, q_cross, keys, values = (ref[...] for ref in refs[:4])
    video_keys = keys.shape[0] // n_tower * (n_tower - 1)
    video_queries = q_self.shape[0] // n_tower * (n_tower - 1)
    to_video = jnp.concatenate([q_self[:video_queries], q_cross[video_queries:]], axis=0)
    to_audio = jnp.concatenate([q_cross[:video_queries], q_self[video_queries:]], axis=0)
    last_video = pl.cdiv(video_keys, DHEAD) * DHEAD
    first_audio = video_keys // DHEAD * DHEAD
    video, video_sum = attend(
        to_video, keys[:last_video], values[:last_video], bias_ref[0:1, :last_video]
    )
    audio, audio_sum = attend(
        to_audio, keys[first_audio:], values[first_audio:], bias_ref[1:2, first_audio:]
    )
    combined = video * audio_sum + audio * video_sum
    combined = (combined * (kept_ref[...] / (video_sum * audio_sum))).astype(jnp.bfloat16)
    for device in range(devices):
        out_ref[ranks[1][device]] = combined[device * block_rows : (device + 1) * block_rows]


def norm_scale(blocks_ref):
    heads, tokens, _ = blocks_ref.shape
    total = jnp.zeros((tokens, DHEAD), jnp.float32)
    for head in range(heads):
        block = blocks_ref[head].astype(jnp.float32)
        total += block * block
    mean = jnp.sum(total, axis=1, keepdims=True) * (1.0 / (heads * DHEAD))
    return lax.rsqrt(mean + 1e-6)


def half_ranks(head_ranks):
    half_heads = len(head_ranks) // 2
    first = lax.axis_index("cfg") == 0
    return [
        jnp.where(first, head_ranks[at], head_ranks[half_heads + at]) for at in range(half_heads)
    ]


def norm_kernel(head_ranks, blocks_ref, kept_ref):
    scale = norm_scale(blocks_ref)
    for at, rank in enumerate(half_ranks(head_ranks)):
        normed = blocks_ref[rank].astype(jnp.float32) * scale
        kept_ref[:, at * DHEAD : (at + 1) * DHEAD] = normed.astype(jnp.bfloat16)


def guide_kernel(head_ranks, guidance_ref, kept_ref, met_ref, out_ref):
    scale = norm_scale(met_ref)
    first = lax.axis_index("cfg") == 0
    guidance = guidance_ref[0]
    for at, rank in enumerate(half_ranks(head_ranks)):
        columns = slice(at * DHEAD, (at + 1) * DHEAD)
        kept = kept_ref[:, columns].astype(jnp.float32)
        met = (met_ref[rank].astype(jnp.float32) * scale).astype(jnp.bfloat16).astype(jnp.float32)
        conditional, unconditional = jnp.where(first, kept, met), jnp.where(first, met, kept)
        guided = unconditional + guidance * (conditional - unconditional)
        out_ref[:, columns] = guided.astype(jnp.bfloat16)


def local_call(kernel, out_shape, in_spaces, arrays, scratch=()):
    out_spec = pl.BlockSpec(memory_space=pltpu.VMEM)
    return pl.pallas_call(
        kernel,
        out_shape=out_shape,
        in_specs=[pl.BlockSpec(memory_space=space) for space in in_spaces],
        out_specs=[out_spec] * len(out_shape) if isinstance(out_shape, list) else out_spec,
        scratch_shapes=scratch,
        compiler_params=pltpu.CompilerParams(vmem_limit_bytes=VMEM_LIMIT),
    )(
        *(
            pltpu.with_memory_space_constraint(array, space) if space == pltpu.HBM else array
            for array, space in zip(arrays, in_spaces)
        )
    )


def per_device(query_self, query_cross, key_vectors, values, positions, counts, guidance):
    n_tower, n_seq = lax.axis_size("tower"), lax.axis_size("seq")
    devices = n_tower * n_seq
    tokens, features = query_self.shape[1:]
    query_blocks = devices // HEADS
    block_rows = tokens // query_blocks
    video_keys = (n_tower - 1) * n_seq * tokens
    spreading, collecting = list(range(devices)), list(range(devices))
    if query_blocks == 1:
        spreading = [devices - 1 - at // 2 if at % 2 == 0 else at // 2 for at in range(devices)]
        middle = devices - n_seq - 1
        collecting = [middle] + [device for device in spreading if device != middle]
    ranks = [[order.index(device) for device in range(devices)] for order in (spreading, collecting)]

    def exchange(array, order):
        return lax.all_to_all(
            array,
            ("tower", "seq"),
            split_axis=0,
            concat_axis=0,
            tiled=True,
            axis_index_groups=[order],
        )

    packed, bias, kept_rows = local_call(
        functools.partial(rotate_kernel, video_keys),
        [
            pltpu.VMEM((HEADS, 4 * tokens, DHEAD), jnp.bfloat16),
            pltpu.VMEM((2, devices * tokens), jnp.float32),
            pltpu.VMEM((devices * block_rows, DHEAD), jnp.float32),
        ],
        [pltpu.HBM] * 6,
        (positions, counts, query_self, query_cross, key_vectors, values),
        [
            pltpu.VMEM((4, tokens, features), jnp.bfloat16),
            pltpu.SMEM((tokens,), jnp.int32),
            pltpu.SMEM((devices,), jnp.int32),
            pltpu.SemaphoreType.DMA((6,)),
        ],
    )
    if query_blocks == 1:
        arrived = [exchange(packed, spreading)]
    else:
        packed = packed.reshape(HEADS, 4, tokens, DHEAD)
        queries = packed[:, :2].reshape(HEADS, 2, query_blocks, block_rows, DHEAD)
        queries = queries.transpose(0, 2, 1, 3, 4).reshape(devices, 2, block_rows, DHEAD)
        spread = jnp.broadcast_to(packed[:, None, 2:], (HEADS, query_blocks, 2, tokens, DHEAD))
        spread = spread.reshape(devices, 2, tokens, DHEAD)
        arrived = [
            exchange(part, spreading).transpose(1, 0, 2, 3).reshape(2, -1, DHEAD)
            for part in (queries, spread)
        ]
        arrived = [part[at] for part in arrived for at in range(2)]
    blocks = local_call(
        functools.partial(attend_kernel, n_tower, ranks),
        pltpu.VMEM((devices, block_rows, DHEAD), jnp.bfloat16),
        [pltpu.VMEM] * (2 + len(arrived)),
        (bias, kept_rows, *arrived),
    )
    half = (tokens, features // 2)
    returned = exchange(blocks, collecting).reshape(HEADS, tokens, DHEAD)
    workers = spreading if query_blocks == 1 else list(range(HEADS))
    head_ranks = [ranks[1][worker] for worker in workers]
    met = lax.ppermute(returned, "cfg", [(0, 1), (1, 0)])
    kept = local_call(
        functools.partial(norm_kernel, head_ranks),
        pltpu.VMEM(half, jnp.bfloat16),
        [pltpu.VMEM],
        (returned,),
    )
    return local_call(
        functools.partial(guide_kernel, head_ranks),
        jax.ShapeDtypeStruct(half, jnp.bfloat16),
        [pltpu.SMEM, pltpu.VMEM, pltpu.VMEM],
        (guidance, kept, met),
    )


def solution(mesh):
    return jax.shard_map(
        per_device,
        mesh=mesh,
        in_specs=(
            P("cfg", ("tower", "seq"), None),
            P("cfg", ("tower", "seq"), None),
            P("cfg", ("tower", "seq"), None),
            P("cfg", ("tower", "seq"), None),
            P(("tower", "seq")),
            P(),
            P(),
        ),
        out_specs=P(("tower", "seq"), "cfg"),
        check_vma=False,
    )
```
